32 devices in a mesh: seq: 8 (over z, y), tp: 4 (over x, core).
Axes of the slice: x: 2, y: 2, z: 4, core: 2. Of those that a mesh axis runs over, the one named last changes fastest.
Arguments:
- features: bfloat16 [2048, 3, 4096], P('seq', None, 'tp'), may hold values from -6 to 6
- short_taps: float32 [3, 7, 4096], P(None, None, 'tp'), may hold values from -2 to 2
- residue: float32 [16, 4096], P(None, 'tp'), may hold values from -1.5 to 1.5
- decay_rate: float32 [16, 4096], P(None, 'tp'), may hold values from 4.8828126e-05 to 0.05
- w_out: bfloat16 [4096, 4096], P('tp', 'seq'), may hold values from -0.09375 to 0.09375
- cotangent: bfloat16 [2048, 4096], P('seq', 'tp'), may hold values from -6 to 6
Outputs:
- mixed: bfloat16 [2048, 4096], P('seq', 'tp')
- grad_features: bfloat16 [2048, 3, 4096], P('seq', None, 'tp')
- grad_weight: float32 [4096, 4096], P('tp', 'seq')
- grad_taps: float32 [3, 7, 4096], P(None, None, 'tp')
- grad_residue: float32 [16, 4096], P(None, 'tp')
- grad_log_rate: float32 [16, 4096], P(None, 'tp')
The draws below stay inside these ranges and needn't reach their ends.
All inputs are finite; a program needn't handle non-finite values.
Results may differ from the reference program's by a relative error of at most 0.013.
Values may be sent and summed in bfloat16 or wider, within the bound.
A program may use at most 128 MiB of HBM per device.

```python
import math
import jax
import jax.numpy as jnp
from jax import lax

D = 4096
MODES = 16
TAPS = 7
TOKENS = 2048
N_TP = 4


def with_spikes(array, rng, source, target, parts, factor):
    owner, partner = [(jnp.arange(array.shape[position]) // (array.shape[position] // parts)).reshape([-1 if axis == position else 1 for axis in range(array.ndim)]) for position in (source, target)]
    chosen = jax.random.permutation(rng, parts)[partner]
    strong = (owner == chosen) | (owner == (partner + parts // 2) % parts)
    return jnp.where(strong, factor * array, array)


def block_levels(key, extent, shards, low, top_value):
    factor_of, own = 1.0, jax.random.fold_in(key, 6)
    for dim, blocks in shards:
        draws = jnp.exp(jax.random.uniform(jax.random.fold_in(own, dim), (blocks,), jnp.float32, low / len(shards), top_value / len(shards)))
        factor_of = factor_of * jnp.repeat(draws, extent[dim] // blocks).reshape([-1 if axis == dim else 1 for axis in range(len(extent))])
    return factor_of


def normal_values(rng, shape, scale, limit, split=(), kind=jnp.bfloat16):
    entries = scale * jax.random.normal(rng, shape, jnp.float32)
    if split:
        entries = entries * block_levels(rng, shape, split, -0.22, 0.18)
    return jnp.clip(entries, -limit, limit).astype(kind)


def noise_with(stream_key, dims, deviation, most, shards, heavy, kind=jnp.bfloat16):
    drawn = deviation * jax.random.normal(stream_key, dims, jnp.float32)
    if shards:
        drawn = drawn * block_levels(stream_key, dims, shards, -0.22, 0.18)
    return jnp.clip(with_spikes(drawn, jax.random.fold_in(stream_key, 3), *heavy), -most, most).astype(kind)


def setup_inputs(seed: int = 0) -> dict:
    seeds = jax.random.split(jax.random.key(seed), 7)
    features = normal_values(seeds[0], (TOKENS, 3, D), 1.0, 6.0, ((0, 8), (2, 4)))
    short_taps = normal_values(seeds[1], (3, TAPS, D), TAPS ** -0.5, 2.0, ((2, 4),), jnp.float32)
    residue = normal_values(seeds[2], (MODES, D), MODES ** -0.5, 1.5, ((1, 4),), jnp.float32)
    decay_rate = jnp.clip(jnp.exp(math.log(0.05) - 6.931472 * jax.random.uniform(seeds[3], (MODES, D), jnp.float32) ** block_levels(seeds[3], (MODES, D), ((1, 4),), -0.2, 0.2)), 4.882812572759576e-05, 0.05)
    w_out = normal_values(seeds[4], (D, D), D ** -0.5, 0.09375, ((0, 4), (1, 8)))
    cotangent = noise_with(seeds[5], (TOKENS, D), 1.0, 6.0, ((0, 8), (1, 4)), (0, 1, 8, 2.0))
    return {"features": features, "short_taps": short_taps, "residue": residue, "decay_rate": decay_rate, "w_out": w_out, "cotangent": cotangent}


def short_conv(stream, taps):
    tok_total = stream.shape[0]
    tap_reach = taps.shape[0] - 1
    padded = jnp.pad(stream, ((tap_reach, 0), (0, 0)))
    result = taps[0] * stream.astype(jnp.float32)
    for tap_index in range(1, tap_reach + 1):
        result = result + taps[tap_index] * padded[tap_reach - tap_index:tap_reach - tap_index + tok_total].astype(jnp.float32)
    return result

def short_conv_back(grads, stream, taps):
    tok_total = grads.shape[0]
    tap_reach = taps.shape[0] - 1
    grads_wide = grads.astype(jnp.float32)
    stream_wide = stream.astype(jnp.float32)
    ahead = jnp.pad(grads_wide, ((0, tap_reach), (0, 0)))
    behind = jnp.pad(stream_wide, ((tap_reach, 0), (0, 0)))
    result = taps[0] * grads_wide
    tap_rows = [jnp.einsum('tc,tc->c', grads_wide, stream_wide)]
    for tap_index in range(1, tap_reach + 1):
        result = result + taps[tap_index] * ahead[tap_index:tap_index + tok_total]
        tap_rows.append(jnp.einsum('tc,tc->c', grads_wide, behind[tap_reach - tap_index:tap_reach - tap_index + tok_total]))
    return (result.astype(jnp.bfloat16), jnp.stack(tap_rows, axis=0))

def block_conv(signal, residue, rate):
    length = signal.shape[1]
    lag_values = jnp.arange(length, dtype=jnp.float32)
    coeffs = residue * jnp.sqrt(-jnp.expm1(-2.0 * rate))
    kernel = lax.optimization_barrier(jnp.sum(coeffs[:, :, None] * jnp.exp(-rate[:, :, None] * lag_values[None, None, :]), axis=0))
    padded_len = 2 * length
    spectrum = jnp.fft.rfft(signal, n=padded_len) * jnp.fft.rfft(kernel, n=padded_len)
    return jnp.fft.irfft(spectrum, n=padded_len)[:, :length]

def block_step(inputs):
    signal, upstream, residue, rate = inputs
    output, pullback = jax.vjp(block_conv, signal, residue, rate)
    grad_signal, grad_res, grad_rate = pullback(upstream)
    return (output, grad_signal, grad_res, grad_rate)

def split_channels(matrix, block_width):
    leading = matrix.shape[0]
    return jnp.transpose(matrix.reshape(leading, -1, block_width), (1, 0, 2))

def join_channels(blocks):
    return jnp.transpose(blocks, (1, 0, 2)).reshape(blocks.shape[1], -1)

def reference(features, short_taps, residue, decay_rate, w_out, cotangent):
    tok_total = features.shape[0]
    channel_count = features.shape[2]
    query_part = short_conv(features[:, 0, :], short_taps[0])
    keyed = short_conv(features[:, 1, :], short_taps[1])
    valued = short_conv(features[:, 2, :], short_taps[2])
    product = (keyed * valued).astype(jnp.bfloat16)
    grad_gated = jnp.dot(cotangent, w_out.T, preferred_element_type=jnp.float32).astype(jnp.bfloat16)
    grad_conv = (grad_gated * query_part).astype(jnp.bfloat16)
    block_width = min(64, channel_count)
    sig_blocks = product.T.astype(jnp.float32).reshape(-1, block_width, tok_total)
    up_blocks = grad_conv.T.astype(jnp.float32).reshape(-1, block_width, tok_total)
    conv_blocks, grad_blocks, res_blocks, rate_blocks = lax.map(block_step, (sig_blocks, up_blocks, split_channels(residue, block_width), split_channels(decay_rate, block_width)))
    convolved = conv_blocks.reshape(channel_count, tok_total).T.astype(jnp.bfloat16)
    grad_product = grad_blocks.reshape(channel_count, tok_total).T.astype(jnp.bfloat16)
    grad_residue = join_channels(res_blocks)
    grad_log_rate = join_channels(rate_blocks) * decay_rate
    gated = (query_part * convolved).astype(jnp.bfloat16)
    group_width = channel_count // N_TP
    mixed_total = jnp.zeros((tok_total, channel_count), jnp.float32)
    for group_index in range(N_TP):
        lower_edge = group_index * group_width
        partial_out = jnp.dot(gated[:, lower_edge:lower_edge + group_width], w_out[lower_edge:lower_edge + group_width], preferred_element_type=jnp.float32)
        rounded = lax.optimization_barrier(partial_out.astype(jnp.bfloat16))
        mixed_total = mixed_total + rounded.astype(jnp.float32)
    mixed = mixed_total.astype(jnp.bfloat16)
    grad_weight = jnp.dot(gated.T, cotangent, preferred_element_type=jnp.float32)
    grad_query = (grad_gated * convolved).astype(jnp.bfloat16)
    grad_key = (grad_product * valued).astype(jnp.bfloat16)
    grad_value = (grad_product * keyed).astype(jnp.bfloat16)
    feat_query, taps_query = short_conv_back(grad_query, features[:, 0, :], short_taps[0])
    feat_key, taps_key = short_conv_back(grad_key, features[:, 1, :], short_taps[1])
    feat_value, taps_value = short_conv_back(grad_value, features[:, 2, :], short_taps[2])
    grad_features = jnp.stack([feat_query, feat_key, feat_value], axis=1)
    grad_taps = jnp.stack([taps_query, taps_key, taps_value], axis=0)
    return (mixed, grad_features, grad_weight, grad_taps, grad_residue, grad_log_rate)
```

```python
import jax
import jax.numpy as jnp
from jax import lax
from jax.experimental import pallas as pl
from jax.experimental.pallas import tpu as pltpu
from jax.sharding import PartitionSpec as P


def shifted(array, axis, by):
    devices = lax.axis_size(axis)
    pairs = [(i, i + by) for i in range(devices) if 0 <= i + by < devices]
    return lax.ppermute(array, axis, pairs)


GROUP = 16


def token_block(tokens):
    return min(256, tokens)


def row_total(terms):
    return jnp.sum(terms, axis=0, keepdims=True)


def forward_kernel(x_ref, decay_ref, coeff_ref, out_ref, entry_ref, state_ref):
    @pl.when(pl.program_id(0) == 0)
    def _():
        state_ref[...] = jnp.zeros_like(state_ref)

    entry_ref[0] = state_ref[...]
    decay = decay_ref[...]
    coeff = coeff_ref[...]

    def step(group, state):
        rows = pl.ds(pl.multiple_of(group * GROUP, GROUP), GROUP)
        x_rows = x_ref[rows, :].astype(jnp.float32)
        outs = []
        for j in range(GROUP):
            state = decay * state + x_rows[j : j + 1, :]
            outs.append(row_total(coeff * state))
        out_ref[rows, :] = jnp.concatenate(outs, axis=0).astype(out_ref.dtype)
        return state

    state_ref[...] = lax.fori_loop(0, x_ref.shape[0] // GROUP, step, state_ref[...])


def backward_kernel(
    x_ref, g_ref, entry_ref, decay_ref, coeff_ref, out_ref, alpha_ref, beta_ref, adj_ref, before_ref
):
    @pl.when(pl.program_id(0) == 0)
    def _():
        adj_ref[...] = jnp.zeros_like(adj_ref)
        alpha_ref[...] = jnp.zeros_like(alpha_ref)
        beta_ref[...] = jnp.zeros_like(beta_ref)

    decay = decay_ref[...]
    coeff = coeff_ref[...]
    groups = x_ref.shape[0] // GROUP

    def states(group, carry):
        state, alpha = carry
        first = pl.multiple_of(group * GROUP, GROUP)
        x_rows = x_ref[pl.ds(first, GROUP), :].astype(jnp.float32)
        g_rows = g_ref[pl.ds(first, GROUP), :].astype(jnp.float32)
        for j in range(GROUP):
            before_ref[first + j] = state
            state = decay * state + x_rows[j : j + 1, :]
            alpha = alpha + g_rows[j : j + 1, :] * state
        return (state, alpha)

    _, alpha = lax.fori_loop(0, groups, states, (entry_ref[0], alpha_ref[...]))
    alpha_ref[...] = alpha

    def adjoints(index, carry):
        adjoint, beta = carry
        first = pl.multiple_of((groups - 1 - index) * GROUP, GROUP)
        g_rows = g_ref[pl.ds(first, GROUP), :].astype(jnp.float32)
        outs = [None] * GROUP
        for j in range(GROUP - 1, -1, -1):
            adjoint = decay * adjoint + g_rows[j : j + 1, :]
            beta = beta + adjoint * before_ref[first + j]
            outs[j] = row_total(coeff * adjoint)
        out_ref[pl.ds(first, GROUP), :] = jnp.concatenate(outs, axis=0).astype(out_ref.dtype)
        return (adjoint, beta)

    adjoint, beta = lax.fori_loop(0, groups, adjoints, (adj_ref[...], beta_ref[...]))
    adj_ref[...] = adjoint
    beta_ref[...] = beta


def modal_output(signal, decay, coeffs):
    tokens, channels = signal.shape
    modes = decay.shape[0]
    block = token_block(tokens)
    blocks = tokens // block
    fixed = pl.BlockSpec((modes, channels), lambda i: (0, 0))
    return pl.pallas_call(
        forward_kernel,
        grid=(blocks,),
        in_specs=[pl.BlockSpec((block, channels), lambda i: (i, 0)), fixed, fixed],
        out_specs=[
            pl.BlockSpec((block, channels), lambda i: (i, 0)),
            pl.BlockSpec((1, modes, channels), lambda i: (i, 0, 0)),
        ],
        out_shape=[
            jax.ShapeDtypeStruct((tokens, channels), jnp.bfloat16),
            jax.ShapeDtypeStruct((blocks, modes, channels), jnp.float32),
        ],
        scratch_shapes=[pltpu.VMEM((modes, channels), jnp.float32)],
        cost_estimate=pl.CostEstimate(
            flops=tokens * modes * channels * 3000,
            bytes_accessed=tokens * channels * 4,
            transcendentals=0,
        ),
        name="modal_forward",
    )(signal, decay, coeffs)


def modal_grads(signal, upstream, entries, decay, coeffs):
    tokens, channels = signal.shape
    modes = decay.shape[0]
    block = token_block(tokens)
    blocks = tokens // block
    fixed = pl.BlockSpec((modes, channels), lambda i: (0, 0))
    rows = pl.BlockSpec((block, channels), lambda i: (blocks - 1 - i, 0))
    return pl.pallas_call(
        backward_kernel,
        grid=(blocks,),
        in_specs=[
            rows,
            rows,
            pl.BlockSpec((1, modes, channels), lambda i: (blocks - 1 - i, 0, 0)),
            fixed,
            fixed,
        ],
        out_specs=[rows, fixed, fixed],
        out_shape=[
            jax.ShapeDtypeStruct((tokens, channels), jnp.bfloat16),
            jax.ShapeDtypeStruct((modes, channels), jnp.float32),
            jax.ShapeDtypeStruct((modes, channels), jnp.float32),
        ],
        scratch_shapes=[
            pltpu.VMEM((modes, channels), jnp.float32),
            pltpu.VMEM((block, modes, channels), jnp.float32),
        ],
        cost_estimate=pl.CostEstimate(
            flops=tokens * modes * channels * 5000,
            bytes_accessed=tokens * channels * 6,
            transcendentals=0,
        ),
        name="modal_backward",
    )(signal, upstream, entries, decay, coeffs)


def coef_grads(alpha_rows, beta_rows, rates, residue):
    scales = jnp.sqrt(-jnp.expm1(-2.0 * rates))
    grad_res = scales * alpha_rows
    grad_log = rates * (
        alpha_rows * residue * jnp.exp(-2.0 * rates) / scales
        - jnp.exp(-rates) * residue * scales * beta_rows
    )
    return (grad_res, grad_log)


def local(features, short_taps, residue, decay_rate, w_out, cotangent):
    tok_count = features.shape[0]
    tap_reach = short_taps.shape[1] - 1
    earlier = shifted(features[tok_count - tap_reach :], "seq", 1)
    extended = jnp.concatenate([earlier, features], axis=0)
    mixed_in = short_taps[:, 0, :] * features
    for tap_index in range(1, tap_reach + 1):
        mixed_in = (
            mixed_in
            + short_taps[:, tap_index, :]
            * extended[tap_reach - tap_index : tap_reach - tap_index + tok_count]
        )
    query_part = mixed_in[:, 0, :]
    keyed = mixed_in[:, 1, :]
    valued = mixed_in[:, 2, :]
    product = (keyed * valued).astype(jnp.bfloat16)
    coeffs = residue * jnp.sqrt(-jnp.expm1(-2.0 * decay_rate))
    mode_count = residue.shape[0]
    chan_share = product.shape[1] // lax.axis_size("seq")
    first_channel = lax.axis_index("seq") * chan_share
    local_rates = lax.dynamic_slice_in_dim(decay_rate, first_channel, chan_share, 1)
    local_coeffs = lax.dynamic_slice_in_dim(coeffs, first_channel, chan_share, 1)
    local_residue = lax.dynamic_slice_in_dim(residue, first_channel, chan_share, 1)
    local_decay = jnp.exp(-local_rates)
    seq_count = lax.axis_size("seq")
    full_weight = lax.all_gather(w_out, "seq", axis=1, tiled=True)
    grad_rows = lax.all_gather(cotangent, "tp", axis=1, tiled=True)
    by_channel = lax.all_to_all(product, "seq", split_axis=1, concat_axis=0, tiled=True)
    conv_channels, entries = modal_output(by_channel, local_decay, local_coeffs)
    convolved = lax.all_to_all(conv_channels, "seq", split_axis=0, concat_axis=1, tiled=True)
    gated = (query_part * convolved).astype(jnp.bfloat16)
    quarter = lax.all_to_all(cotangent, "tp", split_axis=0, concat_axis=1, tiled=True)
    quarter = lax.all_to_all(quarter, "seq", split_axis=1, concat_axis=0, tiled=True)
    full_weight, gated, quarter = lax.optimization_barrier((full_weight, gated, quarter))
    half = gated.shape[1] // 2
    gated_first = lax.all_gather(gated[:, :half], "seq", axis=0, tiled=True)
    gated_second = lax.all_gather(gated[:, half:], "seq", axis=0, tiled=True)
    cot_columns = lax.all_gather(quarter, "tp", axis=0)
    grad_gated = lax.dot_general(
        grad_rows, full_weight, (((1,), (1,)), ((), ())), preferred_element_type=jnp.float32
    ).astype(jnp.bfloat16)
    grad_conv = (grad_gated * query_part).astype(jnp.bfloat16)
    partial_out = jnp.dot(gated, full_weight, preferred_element_type=jnp.float32).astype(
        jnp.bfloat16
    )
    grad_conv, partial_out = lax.optimization_barrier((grad_conv, partial_out))
    mixed = lax.psum_scatter(partial_out, "tp", scatter_dimension=1, tiled=True)
    grad_channels = lax.all_to_all(grad_conv, "seq", split_axis=1, concat_axis=0, tiled=True)
    back_channels, alpha_rows, beta_rows = modal_grads(
        by_channel, grad_channels, entries, local_decay, local_coeffs
    )
    local_res, local_log = coef_grads(alpha_rows, beta_rows, local_rates, local_residue)
    mode_rows = jnp.concatenate([local_res, local_log], axis=0).astype(jnp.bfloat16)
    sent = jnp.concatenate(
        [
            back_channels.reshape(seq_count, tok_count, chan_share),
            jnp.broadcast_to(mode_rows, (seq_count, 2 * mode_count, chan_share)),
        ],
        axis=1,
    )
    received = lax.all_to_all(sent, "seq", split_axis=0, concat_axis=0, tiled=True)
    received, gated_first, cot_columns = lax.optimization_barrier(
        (received, gated_first, cot_columns)
    )
    received = received.transpose(1, 0, 2).reshape(tok_count + 2 * mode_count, -1)
    grad_product = received[:tok_count]
    grad_residue = received[tok_count : tok_count + mode_count].astype(jnp.float32)
    grad_log_rate = received[tok_count + mode_count :].astype(jnp.float32)
    grad_query = grad_gated * convolved
    grad_key = (grad_product * valued).astype(jnp.bfloat16)
    grad_value = (grad_product * keyed).astype(jnp.bfloat16)
    grad_mixed_in = jnp.stack([grad_query, grad_key, grad_value], axis=1)
    later_rows = shifted(grad_mixed_in[:tap_reach], "seq", -1)
    grad_ext = jnp.concatenate([grad_mixed_in, later_rows], axis=0)
    grad_feat = short_taps[:, 0, :] * grad_mixed_in
    tap_terms = [
        jnp.einsum("tjc,tjc->jc", grad_mixed_in, features, preferred_element_type=jnp.float32)
    ]
    for tap_index in range(1, tap_reach + 1):
        grad_feat = (
            grad_feat + short_taps[:, tap_index, :] * grad_ext[tap_index : tap_index + tok_count]
        )
        tap_terms.append(
            jnp.einsum(
                "tjc,tjc->jc",
                grad_mixed_in,
                extended[tap_reach - tap_index : tap_reach - tap_index + tok_count],
                preferred_element_type=jnp.float32,
            )
        )
    tap_local = jnp.stack(tap_terms, axis=1)
    grad_taps = lax.psum(tap_local, "seq")
    tp_count = lax.axis_size("tp")
    cot_columns = (
        cot_columns.reshape(tp_count, seq_count, tok_count // tp_count, -1)
        .transpose(1, 0, 2, 3)
        .reshape(seq_count * tok_count, -1)
    )
    grad_feat = grad_feat.astype(jnp.bfloat16)
    gated_second, _ = lax.optimization_barrier((gated_second, grad_feat))
    grad_weight = jnp.concatenate(
        [
            lax.dot_general(
                rows, cot_columns, (((0,), (0,)), ((), ())), preferred_element_type=jnp.float32
            )
            for rows in (gated_first, gated_second)
        ],
        axis=0,
    )
    return (
        mixed,
        grad_feat,
        grad_weight,
        grad_taps,
        grad_residue,
        grad_log_rate,
    )


def solution(mesh):
    return jax.shard_map(
        local,
        mesh=mesh,
        in_specs=(
            P("seq", None, "tp"),
            P(None, None, "tp"),
            P(None, "tp"),
            P(None, "tp"),
            P("tp", "seq"),
            P("seq", "tp"),
        ),
        out_specs=(
            P("seq", "tp"),
            P("seq", None, "tp"),
            P("tp", "seq"),
            P(None, None, "tp"),
            P(None, "tp"),
            P(None, "tp"),
        ),
        check_vma=False,
    )
```

```python
import jax
import jax.numpy as jnp
from jax import lax
from jax.experimental import pallas as pl
from jax.experimental.pallas import tpu as pltpu
from jax.sharding import PartitionSpec as P


def shifted(array, axis, by):
    devices = lax.axis_size(axis)
    pairs = [(i, i + by) for i in range(devices) if 0 <= i + by < devices]
    return lax.ppermute(array, axis, pairs)


GROUP = 16


def token_block(tokens):
    return min(256, tokens)


def row_total(terms):
    return jnp.sum(terms, axis=0, keepdims=True)


def forward_kernel(x_ref, decay_ref, coeff_ref, out_ref, entry_ref, state_ref):
    @pl.when(pl.program_id(0) == 0)
    def _():
        state_ref[...] = jnp.zeros_like(state_ref)

    entry_ref[0] = state_ref[...]
    decay = decay_ref[...]
    coeff = coeff_ref[...]

    def step(group, state):
        rows = pl.ds(pl.multiple_of(group * GROUP, GROUP), GROUP)
        x_rows = x_ref[rows, :].astype(jnp.float32)
        outs = []
        for j in range(GROUP):
            state = decay * state + x_rows[j : j + 1, :]
            outs.append(row_total(coeff * state))
        out_ref[rows, :] = jnp.concatenate(outs, axis=0).astype(out_ref.dtype)
        return state

    state_ref[...] = lax.fori_loop(0, x_ref.shape[0] // GROUP, step, state_ref[...])


def backward_kernel(
    x_ref, g_ref, entry_ref, decay_ref, coeff_ref, out_ref, alpha_ref, beta_ref, adj_ref, before_ref
):
    @pl.when(pl.program_id(0) == 0)
    def _():
        adj_ref[...] = jnp.zeros_like(adj_ref)
        alpha_ref[...] = jnp.zeros_like(alpha_ref)
        beta_ref[...] = jnp.zeros_like(beta_ref)

    decay = decay_ref[...]
    coeff = coeff_ref[...]
    groups = x_ref.shape[0] // GROUP

    def states(group, carry):
        state, alpha = carry
        first = pl.multiple_of(group * GROUP, GROUP)
        x_rows = x_ref[pl.ds(first, GROUP), :].astype(jnp.float32)
        g_rows = g_ref[pl.ds(first, GROUP), :].astype(jnp.float32)
        for j in range(GROUP):
            before_ref[first + j] = state
            state = decay * state + x_rows[j : j + 1, :]
            alpha = alpha + g_rows[j : j + 1, :] * state
        return (state, alpha)

    _, alpha = lax.fori_loop(0, groups, states, (entry_ref[0], alpha_ref[...]))
    alpha_ref[...] = alpha

    def adjoints(index, carry):
        adjoint, beta = carry
        first = pl.multiple_of((groups - 1 - index) * GROUP, GROUP)
        g_rows = g_ref[pl.ds(first, GROUP), :].astype(jnp.float32)
        outs = [None] * GROUP
        for j in range(GROUP - 1, -1, -1):
            adjoint = decay * adjoint + g_rows[j : j + 1, :]
            beta = beta + adjoint * before_ref[first + j]
            outs[j] = row_total(coeff * adjoint)
        out_ref[pl.ds(first, GROUP), :] = jnp.concatenate(outs, axis=0).astype(out_ref.dtype)
        return (adjoint, beta)

    adjoint, beta = lax.fori_loop(0, groups, adjoints, (adj_ref[...], beta_ref[...]))
    adj_ref[...] = adjoint
    beta_ref[...] = beta


def modal_output(signal, decay, coeffs):
    tokens, channels = signal.shape
    modes = decay.shape[0]
    block = token_block(tokens)
    blocks = tokens // block
    fixed = pl.BlockSpec((modes, channels), lambda i: (0, 0))
    return pl.pallas_call(
        forward_kernel,
        grid=(blocks,),
        in_specs=[pl.BlockSpec((block, channels), lambda i: (i, 0)), fixed, fixed],
        out_specs=[
            pl.BlockSpec((block, channels), lambda i: (i, 0)),
            pl.BlockSpec((1, modes, channels), lambda i: (i, 0, 0)),
        ],
        out_shape=[
            jax.ShapeDtypeStruct((tokens, channels), jnp.bfloat16),
            jax.ShapeDtypeStruct((blocks, modes, channels), jnp.float32),
        ],
        scratch_shapes=[pltpu.VMEM((modes, channels), jnp.float32)],
        cost_estimate=pl.CostEstimate(
            flops=tokens * modes * channels * 3000,
            bytes_accessed=tokens * channels * 4,
            transcendentals=0,
        ),
        name="modal_forward",
    )(signal, decay, coeffs)


def modal_grads(signal, upstream, entries, decay, coeffs):
    tokens, channels = signal.shape
    modes = decay.shape[0]
    block = token_block(tokens)
    blocks = tokens // block
    fixed = pl.BlockSpec((modes, channels), lambda i: (0, 0))
    rows = pl.BlockSpec((block, channels), lambda i: (blocks - 1 - i, 0))
    return pl.pallas_call(
        backward_kernel,
        grid=(blocks,),
        in_specs=[
            rows,
            rows,
            pl.BlockSpec((1, modes, channels), lambda i: (blocks - 1 - i, 0, 0)),
            fixed,
            fixed,
        ],
        out_specs=[rows, fixed, fixed],
        out_shape=[
            jax.ShapeDtypeStruct((tokens, channels), jnp.bfloat16),
            jax.ShapeDtypeStruct((modes, channels), jnp.float32),
            jax.ShapeDtypeStruct((modes, channels), jnp.float32),
        ],
        scratch_shapes=[
            pltpu.VMEM((modes, channels), jnp.float32),
            pltpu.VMEM((block, modes, channels), jnp.float32),
        ],
        cost_estimate=pl.CostEstimate(
            flops=tokens * modes * channels * 5000,
            bytes_accessed=tokens * channels * 6,
            transcendentals=0,
        ),
        name="modal_backward",
    )(signal, upstream, entries, decay, coeffs)


def coef_grads(alpha_rows, beta_rows, rates, residue):
    scales = jnp.sqrt(-jnp.expm1(-2.0 * rates))
    grad_res = scales * alpha_rows
    grad_log = rates * (
        alpha_rows * residue * jnp.exp(-2.0 * rates) / scales
        - jnp.exp(-rates) * residue * scales * beta_rows
    )
    return (grad_res, grad_log)


def local(features, short_taps, residue, decay_rate, w_out, cotangent):
    tok_count = features.shape[0]
    tap_reach = short_taps.shape[1] - 1
    earlier = shifted(features[tok_count - tap_reach :], "seq", 1)
    extended = jnp.concatenate([earlier, features], axis=0)
    mixed_in = short_taps[:, 0, :] * features
    for tap_index in range(1, tap_reach + 1):
        mixed_in = (
            mixed_in
            + short_taps[:, tap_index, :]
            * extended[tap_reach - tap_index : tap_reach - tap_index + tok_count]
        )
    query_part = mixed_in[:, 0, :]
    keyed = mixed_in[:, 1, :]
    valued = mixed_in[:, 2, :]
    product = (keyed * valued).astype(jnp.bfloat16)
    coeffs = residue * jnp.sqrt(-jnp.expm1(-2.0 * decay_rate))
    mode_count = residue.shape[0]
    chan_share = product.shape[1] // lax.axis_size("seq")
    first_channel = lax.axis_index("seq") * chan_share
    local_rates = lax.dynamic_slice_in_dim(decay_rate, first_channel, chan_share, 1)
    local_coeffs = lax.dynamic_slice_in_dim(coeffs, first_channel, chan_share, 1)
    local_residue = lax.dynamic_slice_in_dim(residue, first_channel, chan_share, 1)
    local_decay = jnp.exp(-local_rates)
    seq_count = lax.axis_size("seq")
    full_weight = lax.all_gather(w_out, "seq", axis=1, tiled=True)
    tp_count = lax.axis_size("tp")
    copies = jnp.broadcast_to(cotangent, (tp_count,) + cotangent.shape)
    grad_rows = lax.all_to_all(copies, "tp", split_axis=0, concat_axis=0, tiled=True)
    grad_rows = grad_rows.transpose(1, 0, 2).reshape(tok_count, -1)
    by_channel = lax.all_to_all(product, "seq", split_axis=1, concat_axis=0, tiled=True)
    conv_channels, entries = modal_output(by_channel, local_decay, local_coeffs)
    convolved = lax.all_to_all(conv_channels, "seq", split_axis=0, concat_axis=1, tiled=True)
    gated = (query_part * convolved).astype(jnp.bfloat16)
    quarter = lax.all_to_all(cotangent, "tp", split_axis=0, concat_axis=1, tiled=True)
    quarter = lax.all_to_all(quarter, "seq", split_axis=1, concat_axis=0, tiled=True)
    full_weight, gated, quarter, grad_rows = lax.optimization_barrier(
        (full_weight, gated, quarter, grad_rows)
    )
    half = gated.shape[1] // 2
    gated_first = lax.all_gather(gated[:, :half], "seq", axis=0, tiled=True)
    gated_second = lax.all_gather(gated[:, half:], "seq", axis=0, tiled=True)
    cot_columns = lax.all_gather(quarter, "tp", axis=0)
    grad_gated = lax.dot_general(
        grad_rows, full_weight, (((1,), (1,)), ((), ())), preferred_element_type=jnp.float32
    ).astype(jnp.bfloat16)
    grad_conv = (grad_gated * query_part).astype(jnp.bfloat16)
    partial_out = jnp.dot(gated, full_weight, preferred_element_type=jnp.float32).astype(
        jnp.bfloat16
    )
    grad_conv, partial_out = lax.optimization_barrier((grad_conv, partial_out))
    grad_channels = lax.all_to_all(grad_conv, "seq", split_axis=1, concat_axis=0, tiled=True)
    back_channels, alpha_rows, beta_rows = modal_grads(
        by_channel, grad_channels, entries, local_decay, local_coeffs
    )
    local_res, local_log = coef_grads(alpha_rows, beta_rows, local_rates, local_residue)
    mode_rows = jnp.concatenate([local_res, local_log], axis=0).astype(jnp.bfloat16)
    sent = jnp.concatenate(
        [
            back_channels.reshape(seq_count, tok_count, chan_share),
            jnp.broadcast_to(mode_rows, (seq_count, 2 * mode_count, chan_share)),
        ],
        axis=1,
    )
    received = lax.all_to_all(sent, "seq", split_axis=0, concat_axis=0, tiled=True)
    received, gated_first, cot_columns, partial_out = lax.optimization_barrier(
        (received, gated_first, cot_columns, partial_out)
    )
    partials = lax.all_to_all(
        partial_out.reshape(tok_count, tp_count, -1).transpose(1, 0, 2),
        "tp",
        split_axis=0,
        concat_axis=0,
        tiled=True,
    )
    mixed = jnp.sum(partials.astype(jnp.float32), axis=0).astype(jnp.bfloat16)
    received = received.transpose(1, 0, 2).reshape(tok_count + 2 * mode_count, -1)
    grad_product = received[:tok_count]
    grad_residue = received[tok_count : tok_count + mode_count].astype(jnp.float32)
    grad_log_rate = received[tok_count + mode_count :].astype(jnp.float32)
    grad_query = grad_gated * convolved
    grad_key = (grad_product * valued).astype(jnp.bfloat16)
    grad_value = (grad_product * keyed).astype(jnp.bfloat16)
    grad_mixed_in = jnp.stack([grad_query, grad_key, grad_value], axis=1)
    later_rows = shifted(grad_mixed_in[:tap_reach], "seq", -1)
    grad_ext = jnp.concatenate([grad_mixed_in, later_rows], axis=0)
    grad_feat = short_taps[:, 0, :] * grad_mixed_in
    tap_terms = [
        jnp.einsum("tjc,tjc->jc", grad_mixed_in, features, preferred_element_type=jnp.float32)
    ]
    for tap_index in range(1, tap_reach + 1):
        grad_feat = (
            grad_feat + short_taps[:, tap_index, :] * grad_ext[tap_index : tap_index + tok_count]
        )
        tap_terms.append(
            jnp.einsum(
                "tjc,tjc->jc",
                grad_mixed_in,
                extended[tap_reach - tap_index : tap_reach - tap_index + tok_count],
                preferred_element_type=jnp.float32,
            )
        )
    tap_local = jnp.stack(tap_terms, axis=1)
    tap_rows = tap_local.shape[0] * tap_local.shape[1]
    pieces = tap_local.reshape(tap_rows, seq_count, chan_share).transpose(1, 0, 2)
    pieces = lax.all_to_all(pieces, "seq", split_axis=0, concat_axis=0, tiled=True)
    tap_sums = jnp.broadcast_to(jnp.sum(pieces, axis=0), (seq_count, tap_rows, chan_share))
    tap_sums = lax.all_to_all(tap_sums, "seq", split_axis=0, concat_axis=0, tiled=True)
    grad_taps = tap_sums.transpose(1, 0, 2).reshape(tap_local.shape)
    cot_columns = (
        cot_columns.reshape(tp_count, seq_count, tok_count // tp_count, -1)
        .transpose(1, 0, 2, 3)
        .reshape(seq_count * tok_count, -1)
    )
    grad_feat = grad_feat.astype(jnp.bfloat16)
    gated_second, _ = lax.optimization_barrier((gated_second, grad_feat))
    grad_weight = jnp.concatenate(
        [
            lax.dot_general(
                rows, cot_columns, (((0,), (0,)), ((), ())), preferred_element_type=jnp.float32
            )
            for rows in (gated_first, gated_second)
        ],
        axis=0,
    )
    return (
        mixed,
        grad_feat,
        grad_weight,
        grad_taps,
        grad_residue,
        grad_log_rate,
    )


def solution(mesh):
    return jax.shard_map(
        local,
        mesh=mesh,
        in_specs=(
            P("seq", None, "tp"),
            P(None, None, "tp"),
            P(None, "tp"),
            P(None, "tp"),
            P("tp", "seq"),
            P("seq", "tp"),
        ),
        out_specs=(
            P("seq", "tp"),
            P("seq", None, "tp"),
            P("tp", "seq"),
            P(None, None, "tp"),
            P(None, "tp"),
            P(None, "tp"),
        ),
        check_vma=False,
    )
```

```python
import jax
import jax.numpy as jnp
from jax import lax
from jax.experimental import pallas as pl
from jax.experimental.pallas import tpu as pltpu
from jax.sharding import PartitionSpec as P


def shifted(array, axis, by):
    devices = lax.axis_size(axis)
    pairs = [(i, i + by) for i in range(devices) if 0 <= i + by < devices]
    return lax.ppermute(array, axis, pairs)


GROUP = 16


def token_block(tokens):
    return min(256, tokens)


def row_total(terms):
    return jnp.sum(terms, axis=0, keepdims=True)


def forward_kernel(x_ref, decay_ref, coeff_ref, out_ref, entry_ref, state_ref):
    @pl.when(pl.program_id(0) == 0)
    def _():
        state_ref[...] = jnp.zeros_like(state_ref)

    entry_ref[0] = state_ref[...]
    decay = decay_ref[...]
    coeff = coeff_ref[...]

    def step(group, state):
        rows = pl.ds(pl.multiple_of(group * GROUP, GROUP), GROUP)
        x_rows = x_ref[rows, :].astype(jnp.float32)
        outs = []
        for j in range(GROUP):
            state = decay * state + x_rows[j : j + 1, :]
            outs.append(row_total(coeff * state))
        out_ref[rows, :] = jnp.concatenate(outs, axis=0).astype(out_ref.dtype)
        return state

    state_ref[...] = lax.fori_loop(0, x_ref.shape[0] // GROUP, step, state_ref[...])


def backward_kernel(
    x_ref, g_ref, entry_ref, decay_ref, coeff_ref, out_ref, alpha_ref, beta_ref, adj_ref, before_ref
):
    @pl.when(pl.program_id(0) == 0)
    def _():
        adj_ref[...] = jnp.zeros_like(adj_ref)
        alpha_ref[...] = jnp.zeros_like(alpha_ref)
        beta_ref[...] = jnp.zeros_like(beta_ref)

    decay = decay_ref[...]
    coeff = coeff_ref[...]
    groups = x_ref.shape[0] // GROUP

    def states(group, carry):
        state, alpha = carry
        first = pl.multiple_of(group * GROUP, GROUP)
        x_rows = x_ref[pl.ds(first, GROUP), :].astype(jnp.float32)
        g_rows = g_ref[pl.ds(first, GROUP), :].astype(jnp.float32)
        for j in range(GROUP):
            before_ref[first + j] = state
            state = decay * state + x_rows[j : j + 1, :]
            alpha = alpha + g_rows[j : j + 1, :] * state
        return (state, alpha)

    _, alpha = lax.fori_loop(0, groups, states, (entry_ref[0], alpha_ref[...]))
    alpha_ref[...] = alpha

    def adjoints(index, carry):
        adjoint, beta = carry
        first = pl.multiple_of((groups - 1 - index) * GROUP, GROUP)
        g_rows = g_ref[pl.ds(first, GROUP), :].astype(jnp.float32)
        outs = [None] * GROUP
        for j in range(GROUP - 1, -1, -1):
            adjoint = decay * adjoint + g_rows[j : j + 1, :]
            beta = beta + adjoint * before_ref[first + j]
            outs[j] = row_total(coeff * adjoint)
        out_ref[pl.ds(first, GROUP), :] = jnp.concatenate(outs, axis=0).astype(out_ref.dtype)
        return (adjoint, beta)

    adjoint, beta = lax.fori_loop(0, groups, adjoints, (adj_ref[...], beta_ref[...]))
    adj_ref[...] = adjoint
    beta_ref[...] = beta


def modal_output(signal, decay, coeffs):
    tokens, channels = signal.shape
    modes = decay.shape[0]
    block = token_block(tokens)
    blocks = tokens // block
    fixed = pl.BlockSpec((modes, channels), lambda i: (0, 0))
    return pl.pallas_call(
        forward_kernel,
        grid=(blocks,),
        in_specs=[pl.BlockSpec((block, channels), lambda i: (i, 0)), fixed, fixed],
        out_specs=[
            pl.BlockSpec((block, channels), lambda i: (i, 0)),
            pl.BlockSpec((1, modes, channels), lambda i: (i, 0, 0)),
        ],
        out_shape=[
            jax.ShapeDtypeStruct((tokens, channels), jnp.bfloat16),
            jax.ShapeDtypeStruct((blocks, modes, channels), jnp.float32),
        ],
        scratch_shapes=[pltpu.VMEM((modes, channels), jnp.float32)],
        cost_estimate=pl.CostEstimate(
            flops=tokens * modes * channels * 3000,
            bytes_accessed=tokens * channels * 4,
            transcendentals=0,
        ),
        name="modal_forward",
    )(signal, decay, coeffs)


def modal_grads(signal, upstream, entries, decay, coeffs):
    tokens, channels = signal.shape
    modes = decay.shape[0]
    block = token_block(tokens)
    blocks = tokens // block
    fixed = pl.BlockSpec((modes, channels), lambda i: (0, 0))
    rows = pl.BlockSpec((block, channels), lambda i: (blocks - 1 - i, 0))
    return pl.pallas_call(
        backward_kernel,
        grid=(blocks,),
        in_specs=[
            rows,
            rows,
            pl.BlockSpec((1, modes, channels), lambda i: (blocks - 1 - i, 0, 0)),
            fixed,
            fixed,
        ],
        out_specs=[rows, fixed, fixed],
        out_shape=[
            jax.ShapeDtypeStruct((tokens, channels), jnp.bfloat16),
            jax.ShapeDtypeStruct((modes, channels), jnp.float32),
            jax.ShapeDtypeStruct((modes, channels), jnp.float32),
        ],
        scratch_shapes=[
            pltpu.VMEM((modes, channels), jnp.float32),
            pltpu.VMEM((block, modes, channels), jnp.float32),
        ],
        cost_estimate=pl.CostEstimate(
            flops=tokens * modes * channels * 5000,
            bytes_accessed=tokens * channels * 6,
            transcendentals=0,
        ),
        name="modal_backward",
    )(signal, upstream, entries, decay, coeffs)


def coef_grads(alpha_rows, beta_rows, rates, residue):
    scales = jnp.sqrt(-jnp.expm1(-2.0 * rates))
    grad_res = scales * alpha_rows
    grad_log = rates * (
        alpha_rows * residue * jnp.exp(-2.0 * rates) / scales
        - jnp.exp(-rates) * residue * scales * beta_rows
    )
    return (grad_res, grad_log)


def local(features, short_taps, residue, decay_rate, w_out, cotangent):
    tok_count = features.shape[0]
    tap_reach = short_taps.shape[1] - 1
    earlier = shifted(features[tok_count - tap_reach :], "seq", 1)
    extended = jnp.concatenate([earlier, features], axis=0)
    mixed_in = short_taps[:, 0, :] * features
    for tap_index in range(1, tap_reach + 1):
        mixed_in = (
            mixed_in
            + short_taps[:, tap_index, :]
            * extended[tap_reach - tap_index : tap_reach - tap_index + tok_count]
        )
    query_part = mixed_in[:, 0, :]
    keyed = mixed_in[:, 1, :]
    valued = mixed_in[:, 2, :]
    product = (keyed * valued).astype(jnp.bfloat16)
    coeffs = residue * jnp.sqrt(-jnp.expm1(-2.0 * decay_rate))
    mode_count = residue.shape[0]
    chan_share = product.shape[1] // lax.axis_size("seq")
    first_channel = lax.axis_index("seq") * chan_share
    local_rates = lax.dynamic_slice_in_dim(decay_rate, first_channel, chan_share, 1)
    local_coeffs = lax.dynamic_slice_in_dim(coeffs, first_channel, chan_share, 1)
    local_residue = lax.dynamic_slice_in_dim(residue, first_channel, chan_share, 1)
    local_decay = jnp.exp(-local_rates)
    seq_count = lax.axis_size("seq")
    full_weight = lax.all_gather(w_out, "seq", axis=1, tiled=True)
    tp_count = lax.axis_size("tp")
    copies = jnp.broadcast_to(cotangent, (tp_count,) + cotangent.shape)
    grad_rows = lax.all_to_all(copies, "tp", split_axis=0, concat_axis=0, tiled=True)
    grad_rows = grad_rows.transpose(1, 0, 2).reshape(tok_count, -1)
    by_channel = lax.all_to_all(product, "seq", split_axis=1, concat_axis=0, tiled=True)
    conv_channels, entries = modal_output(by_channel, local_decay, local_coeffs)
    convolved = lax.all_to_all(conv_channels, "seq", split_axis=0, concat_axis=1, tiled=True)
    gated = (query_part * convolved).astype(jnp.bfloat16)
    quarter = lax.all_to_all(cotangent, "tp", split_axis=0, concat_axis=1, tiled=True)
    quarter = lax.all_to_all(quarter, "seq", split_axis=1, concat_axis=0, tiled=True)
    full_weight, gated, quarter, grad_rows = lax.optimization_barrier(
        (full_weight, gated, quarter, grad_rows)
    )
    half = gated.shape[1] // 2
    gated_first = lax.all_gather(gated[:, :half], "seq", axis=0, tiled=True)
    gated_second = lax.all_gather(gated[:, half:], "seq", axis=0, tiled=True)
    cot_columns = lax.all_gather(quarter, "tp", axis=0)
    grad_gated = lax.dot_general(
        grad_rows, full_weight, (((1,), (1,)), ((), ())), preferred_element_type=jnp.float32
    ).astype(jnp.bfloat16)
    grad_conv = (grad_gated * query_part).astype(jnp.bfloat16)
    partial_out = jnp.dot(gated, full_weight, preferred_element_type=jnp.float32).astype(
        jnp.bfloat16
    )
    grad_channels = lax.all_to_all(grad_conv, "seq", split_axis=1, concat_axis=0, tiled=True)
    back_channels, alpha_rows, beta_rows = modal_grads(
        by_channel, grad_channels, entries, local_decay, local_coeffs
    )
    local_res, local_log = coef_grads(alpha_rows, beta_rows, local_rates, local_residue)
    mode_rows = jnp.concatenate([local_res, local_log], axis=0).astype(jnp.bfloat16)
    sent = jnp.concatenate(
        [
            back_channels.reshape(seq_count, tok_count, chan_share),
            jnp.broadcast_to(mode_rows, (seq_count, 2 * mode_count, chan_share)),
        ],
        axis=1,
    )
    received = lax.all_to_all(sent, "seq", split_axis=0, concat_axis=0, tiled=True)
    received, gated_first, cot_columns, partial_out = lax.optimization_barrier(
        (received, gated_first, cot_columns, partial_out)
    )
    partials = lax.all_to_all(
        partial_out.reshape(tok_count, tp_count, -1).transpose(1, 0, 2),
        "tp",
        split_axis=0,
        concat_axis=0,
        tiled=True,
    )
    received = received.transpose(1, 0, 2).reshape(tok_count + 2 * mode_count, -1)
    grad_product = received[:tok_count]
    grad_residue = received[tok_count : tok_count + mode_count].astype(jnp.float32)
    grad_log_rate = received[tok_count + mode_count :].astype(jnp.float32)
    grad_query = grad_gated * convolved
    grad_key = (grad_product * valued).astype(jnp.bfloat16)
    grad_value = (grad_product * keyed).astype(jnp.bfloat16)
    grad_mixed_in = jnp.stack([grad_query, grad_key, grad_value], axis=1)
    later_rows = shifted(grad_mixed_in[:tap_reach], "seq", -1)
    grad_ext = jnp.concatenate([grad_mixed_in, later_rows], axis=0)
    grad_feat = short_taps[:, 0, :] * grad_mixed_in
    tap_terms = [
        jnp.einsum("tjc,tjc->jc", grad_mixed_in, features, preferred_element_type=jnp.float32)
    ]
    for tap_index in range(1, tap_reach + 1):
        grad_feat = (
            grad_feat + short_taps[:, tap_index, :] * grad_ext[tap_index : tap_index + tok_count]
        )
        tap_terms.append(
            jnp.einsum(
                "tjc,tjc->jc",
                grad_mixed_in,
                extended[tap_reach - tap_index : tap_reach - tap_index + tok_count],
                preferred_element_type=jnp.float32,
            )
        )
    tap_local = jnp.stack(tap_terms, axis=1)
    tap_rows = tap_local.shape[0] * tap_local.shape[1]
    pieces = tap_local.reshape(tap_rows, seq_count, chan_share).transpose(1, 0, 2)
    pieces, partials = lax.optimization_barrier((pieces, partials))
    mixed = jnp.sum(partials.astype(jnp.float32), axis=0).astype(jnp.bfloat16)
    pieces = lax.all_to_all(pieces, "seq", split_axis=0, concat_axis=0, tiled=True)
    tap_sums = jnp.broadcast_to(jnp.sum(pieces, axis=0), (seq_count, tap_rows, chan_share))
    tap_sums = lax.all_to_all(tap_sums, "seq", split_axis=0, concat_axis=0, tiled=True)
    grad_taps = tap_sums.transpose(1, 0, 2).reshape(tap_local.shape)
    cot_columns = (
        cot_columns.reshape(tp_count, seq_count, tok_count // tp_count, -1)
        .transpose(1, 0, 2, 3)
        .reshape(seq_count * tok_count, -1)
    )
    grad_feat = grad_feat.astype(jnp.bfloat16)
    gated_second, _ = lax.optimization_barrier((gated_second, grad_feat))
    grad_weight = jnp.concatenate(
        [
            lax.dot_general(
                rows, cot_columns, (((0,), (0,)), ((), ())), preferred_element_type=jnp.float32
            )
            for rows in (gated_first, gated_second)
        ],
        axis=0,
    )
    return (
        mixed,
        grad_feat,
        grad_weight,
        grad_taps,
        grad_residue,
        grad_log_rate,
    )


def solution(mesh):
    return jax.shard_map(
        local,
        mesh=mesh,
        in_specs=(
            P("seq", None, "tp"),
            P(None, None, "tp"),
            P(None, "tp"),
            P(None, "tp"),
            P("tp", "seq"),
            P("seq", "tp"),
        ),
        out_specs=(
            P("seq", "tp"),
            P("seq", None, "tp"),
            P("tp", "seq"),
            P(None, None, "tp"),
            P(None, "tp"),
            P(None, "tp"),
        ),
        check_vma=False,
    )
```
